32 devices in a mesh: wide: 8 (over y, x, core), narrow: 4 (over z).
Axes of the slice: x: 2, y: 2, z: 4, core: 2. Of those that a mesh axis runs over, the one named last changes fastest.
Arguments:
- tokens: bfloat16 [32768, 384], P(('wide', 'narrow')), may hold values from -6 to 6
- cotangent: bfloat16 [32768, 384], P(('wide', 'narrow')), may hold values from -6 to 6
- segment_ids: int32 [32768], P(('wide', 'narrow')), may hold values from 0 to 1023, as said below
- pad_mask: int32 [32768], P(('wide', 'narrow')), may hold values from 0 to 1, as said below
- bucket: int32 [8], P('wide'), may hold values from 0 to 1, as said below
- loss_weights: int32 [2], replicated, may hold values from 1 to 16
- norm1_gain: float32 [384], replicated, may hold values from 0.1 to 1.9
- norm1_bias: float32 [384], replicated, may hold values from -3 to 3
- qkv_weight: float32 [384, 1152], replicated, may hold values from -0.3125 to 0.3125
- qkv_bias: float32 [1152], replicated, may hold values from -3 to 3
- query_gain: float32 [384], replicated, may hold values from 0.5 to 2
- key_gain: float32 [384], replicated, may hold values from 0.5 to 2
- proj_weight: float32 [384, 384], replicated, may hold values from -2.5 to 2.5
- proj_bias: float32 [384], replicated, may hold values from -3 to 3
- norm2_gain: float32 [384], replicated, may hold values from 0.1 to 1.9
- norm2_bias: float32 [384], replicated, may hold values from -3 to 3
- fc1_weight: float32 [384, 1536], replicated, may hold values from -0.3125 to 0.3125
- fc1_bias: float32 [1536], replicated, may hold values from -3 to 3
- fc2_weight: float32 [1536, 384], replicated, may hold values from -0.15625 to 0.15625
- fc2_bias: float32 [384], replicated, may hold values from -3 to 3
Outputs:
- output: bfloat16 [32768, 384], P(('wide', 'narrow'))
- input_grad: bfloat16 [32768, 384], P(('wide', 'narrow'))
- grad_norm1_gain: float32 [384], replicated
- grad_norm1_bias: float32 [384], replicated
- grad_qkv_weight: float32 [384, 1152], replicated
- grad_qkv_bias: float32 [1152], replicated
- grad_query_gain: float32 [384], replicated
- grad_key_gain: float32 [384], replicated
- grad_proj_weight: float32 [384, 384], replicated
- grad_proj_bias: float32 [384], replicated
- grad_norm2_gain: float32 [384], replicated
- grad_norm2_bias: float32 [384], replicated
- grad_fc1_weight: float32 [384, 1536], replicated
- grad_fc1_bias: float32 [1536], replicated
- grad_fc2_weight: float32 [1536, 384], replicated
- grad_fc2_bias: float32 [384], replicated
The draws below stay inside these ranges and needn't reach their ends.
Inputs may be any that keep to these rules, and one draw needn't show every extreme that they name: Exactly 6 positions of wide are in bucket 0, whose devices hold packs of 1024 positions; the others are in bucket 1, with packs of 256. `segment_ids`: each position's id is the position on its device where its segment begins, so ids never fall along a device; the device is cut into aligned packs of its bucket's size, no segment crosses a pack's border, a pack may end in padding, and the device's last position is a segment of its own. `pad_mask`: 0 exactly on the padding at a pack's end, which holds at most a quarter of the pack.
All inputs are finite; a program needn't handle non-finite values.
Results may differ from the reference program's by a relative error of at most 0.012.
The reference program's roundings to bfloat16 on the way count: a program that leaves them out, or rounds other values in their place, can miss the bound.
Values sent between devices are 32-bit elements; how exact they have to be, the bound alone decides.
A program may use at most 192 MiB of HBM per device.

```python
import math
import jax
import jax.numpy as jnp
from jax import lax

D = 384
FF = 1536
HEADS = 6
HEAD_DIM = 64
TOK_DEV = 1024
PACK_HIGH = 1024
PACK_LOW = 256
TOKENS = 32768
LANES_HIGH = 6
N_WIDE = 8
N_NARROW = 4


def pack_layout(key):
    lanes = jax.random.permutation(jax.random.fold_in(key, 11), N_WIDE)
    bucket = (lanes >= LANES_HIGH).astype(jnp.int32)
    devices = N_WIDE * N_NARROW
    owner = jnp.repeat(bucket, N_NARROW)
    position = jnp.arange(TOK_DEV, dtype=jnp.int32)
    size = jnp.where(owner == 0, PACK_HIGH, PACK_LOW).astype(jnp.int32)[:, None]
    offset = position[None, :] % size
    pack = position[None, :] // size
    rolls = jax.random.randint(jax.random.fold_in(key, 12), (devices, TOK_DEV), 0, size)
    padding = jax.random.randint(jax.random.fold_in(key, 13), (devices, TOK_DEV // PACK_LOW), 0, size // 4 + 1)
    pad_length = jnp.take_along_axis(padding, pack, axis=1)
    used = size - pad_length
    valid = offset < used
    final = position[None, :] == TOK_DEV - 1
    starts = (offset == 0) | (offset == used) | valid & (rolls < 3) | final
    begins = jnp.where(starts, position[None, :], 0).astype(jnp.int32)
    segment = lax.cummax(begins, axis=1)
    return (bucket, segment.reshape(-1).astype(jnp.int32), valid.astype(jnp.int32).reshape(-1))


def draw_bucket(key, part):
    layout = pack_layout(key)
    return layout[0]


def draw_segment_ids(key, part):
    layout = pack_layout(key)
    return layout[1]


def draw_pad_mask(key, part):
    layout = pack_layout(key)
    return layout[2]


def steps_of(key, shape, cuts, low, top_value):
    factor_of, own = 1.0, jax.random.fold_in(key, 6)
    for axis_at, shards_of in cuts:
        draws = jnp.exp(jax.random.uniform(jax.random.fold_in(own, axis_at), (shards_of,), jnp.float32, low / len(cuts), top_value / len(cuts)))
        factor_of = factor_of * jnp.repeat(draws, shape[axis_at] // shards_of).reshape([-1 if axis == axis_at else 1 for axis in range(len(shape))])
    return factor_of


def gaussian(stream_key, extent, scale, reach, pieces=(), held_as=jnp.bfloat16):
    entries = scale * jax.random.normal(stream_key, extent, jnp.float32)
    if pieces:
        entries = entries * steps_of(stream_key, extent, pieces, -0.22, 0.18)
    return jnp.clip(entries, -reach, reach).astype(held_as)


def setup_inputs(seed: int = 0) -> dict:
    key_list = jax.random.split(jax.random.key(seed), 21)
    return {
        "tokens": gaussian(key_list[0], (TOKENS, D), 1.0, 6.0, ((0, 32),)),
        "cotangent": gaussian(key_list[1], (TOKENS, D), 1.0, 6.0, ((0, 32),)),
        "segment_ids": draw_segment_ids(jax.random.fold_in(key_list[20], 71), 0),
        "pad_mask": draw_pad_mask(jax.random.fold_in(key_list[20], 71), 0),
        "bucket": draw_bucket(jax.random.fold_in(key_list[20], 71), 0),
        "loss_weights": jax.random.randint(key_list[5], (2,), 1, 17).astype(jnp.int32),
        "norm1_gain": jnp.clip(1.0 + 0.18 * jax.random.normal(key_list[6], (D,), jnp.float32), 0.1, 1.9),
        "norm1_bias": gaussian(key_list[7], (D,), 0.3, 3.0, (), jnp.float32),
        "qkv_weight": gaussian(key_list[8], (D, 3 * D), D ** -0.5, 0.3125, (), jnp.float32),
        "qkv_bias": gaussian(key_list[9], (3 * D,), 0.3, 3.0, (), jnp.float32),
        "query_gain": jnp.clip(jnp.exp(jax.random.uniform(key_list[10], (D,), jnp.float32, math.log(0.5), math.log(2.0))), 0.5, 2.0),
        "key_gain": jnp.clip(jnp.exp(jax.random.uniform(key_list[11], (D,), jnp.float32, math.log(0.5), math.log(2.0))), 0.5, 2.0),
        "proj_weight": gaussian(key_list[12], (D, D), (max(D // 64, 1)) ** -0.5, 2.5, (), jnp.float32),
        "proj_bias": gaussian(key_list[13], (D,), 0.3, 3.0, (), jnp.float32),
        "norm2_gain": jnp.clip(1.0 + 0.18 * jax.random.normal(key_list[14], (D,), jnp.float32), 0.1, 1.9),
        "norm2_bias": gaussian(key_list[15], (D,), 0.3, 3.0, (), jnp.float32),
        "fc1_weight": gaussian(key_list[16], (D, FF), D ** -0.5, 0.3125, (), jnp.float32),
        "fc1_bias": gaussian(key_list[17], (FF,), 0.3, 3.0, (), jnp.float32),
        "fc2_weight": gaussian(key_list[18], (FF, D), FF ** -0.5, 0.15625, (), jnp.float32),
        "fc2_bias": gaussian(key_list[19], (D,), 0.3, 3.0, (), jnp.float32),
    }


@jax.custom_vjp
def low(v):
    return lax.optimization_barrier(v.astype(jnp.bfloat16)).astype(jnp.float32)

@jax.custom_vjp
def low_back(v):
    return v

def low_keep(v):
    return (low(v), None)

def low_pass(kept, grad):
    return (grad,)

def back_keep(v):
    return (v, None)

def back_low(kept, grad):
    return (low(grad),)
low.defvjp(low_keep, low_pass)
low_back.defvjp(back_keep, back_low)
epsilon = 1e-06
blocked = -1000000000.0
highest = lax.Precision.HIGHEST

def product(left, right):
    return jnp.dot(left, right, precision=highest, preferred_element_type=jnp.float32)

def layer_norm(values, gain, shift):
    center = values - lax.optimization_barrier(jnp.mean(values, -1, keepdims=True))
    spread = lax.optimization_barrier(jnp.mean(center * center, -1, keepdims=True))
    return center * lax.rsqrt(spread + epsilon) * gain + shift

def head_norm(values, gain, factor):
    count = values.shape[0]
    split = values.reshape(count, HEADS, HEAD_DIM)
    center = split - lax.optimization_barrier(jnp.mean(split, -1, keepdims=True))
    spread = lax.optimization_barrier(jnp.mean(center * center, -1, keepdims=True))
    normed = (center * lax.rsqrt(spread + epsilon)).reshape(count, HEADS * HEAD_DIM)
    return normed * gain * factor

def forward(inputs, params, segments):
    norm1_gain, norm1_bias, qkv_weight, qkv_bias, query_gain, key_gain, proj_weight, proj_bias, norm2_gain, norm2_bias, fc1_weight, fc1_bias, fc2_weight, fc2_bias = params
    count = inputs.shape[0]
    width = HEADS * HEAD_DIM
    normed1 = low(layer_norm(inputs, norm1_gain, norm1_bias))
    projected = low_back(product(normed1, low(qkv_weight)) + qkv_bias)
    queries = low(head_norm(projected[:, :width], query_gain, HEAD_DIM ** (-0.5)))
    keys = low(head_norm(projected[:, width:2 * width], key_gain, 1.0))
    values = low(projected[:, 2 * width:])
    scores = jnp.einsum('qhe,khe->hqk', queries.reshape(count, HEADS, HEAD_DIM), keys.reshape(count, HEADS, HEAD_DIM), precision=highest)
    same = segments[:, None] == segments[None, :]
    scores = low_back(jnp.where(same[None], scores, blocked))
    probs = low(jax.nn.softmax(scores, axis=-1))
    mixed = jnp.einsum('hqk,khe->qhe', probs, values.reshape(count, HEADS, HEAD_DIM), precision=highest).reshape(count, width)
    mixed = low(low_back(mixed))
    branch = low_back(product(mixed, low(proj_weight)) + proj_bias)
    middle = inputs + branch
    normed2 = low(layer_norm(middle, norm2_gain, norm2_bias))
    hidden = low_back(product(normed2, low(fc1_weight)) + fc1_bias)
    active = low(jax.nn.gelu(hidden, approximate=False))
    branch2 = low_back(product(active, low(fc2_weight)) + fc2_bias)
    return middle + branch2

def reference(tokens, cotangent, segment_ids, pad_mask, bucket, loss_weights, norm1_gain, norm1_bias, qkv_weight, qkv_bias, query_gain, key_gain, proj_weight, proj_bias, norm2_gain, norm2_bias, fc1_weight, fc1_bias, fc2_weight, fc2_bias):
    params = (norm1_gain, norm1_bias, qkv_weight, qkv_bias, query_gain, key_gain, proj_weight, proj_bias, norm2_gain, norm2_bias, fc1_weight, fc1_bias, fc2_weight, fc2_bias)
    blocks = TOKENS // PACK_HIGH
    per_device = TOK_DEV // PACK_HIGH
    input_blocks = tokens.astype(jnp.float32).reshape(blocks, PACK_HIGH, D)
    upstream = cotangent.astype(jnp.float32) * pad_mask.astype(jnp.float32)[:, None]
    upstream_blocks = upstream.reshape(blocks, PACK_HIGH, D)
    segment_blocks = segment_ids.reshape(blocks, PACK_HIGH)
    device = jnp.arange(blocks, dtype=jnp.int32) // per_device
    lane = device // N_NARROW
    owner = bucket[lane]
    block_weight = jnp.where(owner == 0, loss_weights[0], loss_weights[1]).astype(jnp.float32)

    def step(totals, item):
        block_inputs, block_upstream, block_segments, weight = item
        result, pull = jax.vjp(lambda values, weights: forward(values, weights, block_segments), block_inputs, params)
        grad_inputs, grad_params = pull(block_upstream)
        totals = jax.tree.map(lambda total, grad: total + weight * grad, totals, grad_params)
        return (totals, (result.astype(jnp.bfloat16), grad_inputs.astype(jnp.bfloat16)))
    zeros = jax.tree.map(jnp.zeros_like, params)
    totals, (results, grads) = lax.scan(step, zeros, (input_blocks, upstream_blocks, segment_blocks, block_weight))
    devices = N_WIDE * N_NARROW
    finals = tuple((total / devices for total in totals))
    return (results.reshape(TOKENS, D), grads.reshape(TOKENS, D), finals[0], finals[1], finals[2], finals[3], finals[4], finals[5], finals[6], finals[7], finals[8], finals[9], finals[10], finals[11], finals[12], finals[13])
```

```python
import functools

import jax
import jax.numpy as jnp
from jax import lax
from jax.experimental import pallas as pl
from jax.experimental.pallas import tpu as pltpu
from jax.sharding import PartitionSpec as P

HEADS = 6
HEAD = 64
EPS = 1e-06
CODE = 128.0
LANES = 128
bf16 = jnp.bfloat16
f32 = jnp.float32

NN = ((1,), (0,))
NT = ((1,), (1,))
TN = ((0,), (0,))


def dot(left, right, dims=NN):
    return lax.dot_general(left, right, (dims, ((), ())), preferred_element_type=f32)


def normal_cdf(u):
    z = jnp.abs(u) * 0.7071067811865476
    t = 1.0 / (1.0 + 0.3275911 * z)
    bell = jnp.exp(-(z * z))
    poly = t * (0.254829592 + t * (-0.284496736 + t * (1.421413741 + t * (-1.453152027 + t * 1.061405429))))
    half = 0.5 * poly * bell
    return jnp.where(u < 0, half, 1.0 - half), bell


def layer_kernel(
    tokens, cotangent, seg, mask, bucket, loss_weights,
    n1g, n1b, wqkv, bqkv, gq, gk, wproj, bproj, n2g, n2b, wfc1, bfc1, wfc2, bfc2,
    out, input_grad, g_qkv, g_proj, g_fc1, g_fc2, g_vec,
    w1, w2, wq, wp,
    cols, codes, xT, gmT, n1T, mixT, n2T, gbT, gprT,
    preT, nq, nk, qxT, kxT_n, kT, vxT, vx_n, pT, OT, lT, doT, midT, accT, dn2T, gmidT, dsT,
    stats, rqk, part, sems,
):
    T = tokens.shape[0]
    D = tokens.shape[1]
    FF = wfc1.shape[1]
    NB = FF // D
    NTL = T // LANES
    wq_f, wp_f, w1_f, w2_f = g_qkv, g_proj, g_fc1, g_fc2
    aT, ghT, gpT = dsT.at[:D], dsT.at[D:2 * D], gbT

    def fetch(src, dst, i):
        return pltpu.make_async_copy(src, dst, sems.at[i])

    copies = [
        fetch(wqkv, wq_f, 0), fetch(wproj, wp_f, 1), fetch(wfc1, w1_f, 2), fetch(wfc2, w2_f, 3),
    ]
    for c in copies:
        c.start()

    own = jnp.where(bucket[0] == 0, loss_weights[0], loss_weights[1]).astype(f32)
    devices = lax.axis_size("wide") * lax.axis_size("narrow")
    own = own / devices

    rows = [n1g[...], n1b[...]] + [bqkv[i * D:(i + 1) * D] for i in range(3)] + [gq[...], gk[...], bproj[...], n2g[...], n2b[...]]
    rows += [bfc1[i * D:(i + 1) * D] for i in range(NB)] + [bfc2[...]]
    rows = [v.reshape(1, D) for v in rows]
    N1G, N1B, BQKV, GQ, GK, BP, N2G, N2B, B1 = 0, 1, 2, 5, 6, 7, 8, 9, 10
    B2 = 10 + NB
    stacked = jnp.concatenate(rows + [jnp.zeros((LANES - len(rows), D), f32)], 0)
    colmat = stacked.T
    for j in range(len(rows)):
        cols[j] = jnp.broadcast_to(colmat[:, j:j + 1], (D, LANES))

    segrow = seg[...]
    sub = lax.broadcasted_iota(jnp.int32, (HEAD, T), 0)
    bits = jnp.where((jnp.broadcast_to(segrow, (HEAD, T)) & (1 << jnp.minimum(sub, 12))) != 0, 1.0, -1.0)
    codes[...] = jnp.where(sub < 10, bits, jnp.where(sub == 10, 1.0, 0.0))
    coderow = jnp.where(sub < 10, CODE * bits, jnp.where(sub == 10, -10.0 * CODE, 0.0)).astype(bf16)
    for h in range(HEADS):
        qxT[h, HEAD:, :] = coderow
        vxT[h, HEAD:, :] = jnp.where(lax.broadcasted_iota(jnp.int32, (16, T), 0) == 0, 1.0, 0.0).astype(bf16)

    maskrow = mask[...].astype(f32)
    ones16 = jnp.where(lax.broadcasted_iota(jnp.int32, (16, T), 0) == 0, 1.0, 0.0).astype(bf16)
    n1T[D:, :] = ones16
    n2T[D:, :] = ones16
    mixT[D:, :] = ones16

    inv_d = 1.0 / D

    for t in range(NTL):
        tl = slice(t * LANES, (t + 1) * LANES)
        x = tokens[tl, :].astype(f32).T
        xT[:, tl] = x.astype(bf16)
        mean = jnp.sum(x, 0, keepdims=True) * inv_d
        c = x - mean
        r = lax.rsqrt(jnp.sum(c * c, 0, keepdims=True) * inv_d + EPS)
        n1T[:D, tl] = (c * r * cols[N1G] + cols[N1B]).astype(bf16)
        stats[0:1, tl] = mean
        stats[1:2, tl] = r
        gmT[:, tl] = (cotangent[tl, :].astype(f32).T * maskrow[:, tl]).astype(bf16)

    copies[0].wait()
    wq[...] = wq_f[...].astype(bf16)
    for s in range(3):
        preT[...] = dot(wq[:, s * D:(s + 1) * D], n1T[:D, :], TN)
        ext = jnp.where(lax.broadcasted_iota(jnp.int32, (HEAD, LANES), 0) < 3, 1.0, 0.0)

        def head_loop(t, _):
            tl = pl.ds(pl.multiple_of(t * LANES, LANES), LANES)
            for h in range(HEADS):
                hs = slice(h * HEAD, (h + 1) * HEAD)
                v = preT[hs, tl] + cols[BQKV + s, hs, :]
                if s == 2:
                    vxT[h, :HEAD, tl] = v.astype(bf16)
                    vx_n[h, tl, :] = jnp.concatenate([v, ext], 0).T.astype(bf16)
                    continue
                mean = jnp.sum(v, 0, keepdims=True) * (1.0 / HEAD)
                c = v - mean
                r = lax.rsqrt(jnp.sum(c * c, 0, keepdims=True) * (1.0 / HEAD) + EPS)
                n = c * r
                rqk[s, h, 0:1, tl] = r
                if s == 0:
                    nq[hs, tl] = n
                    qxT[h, :HEAD, tl] = (n * cols[GQ, hs, :] * (HEAD ** -0.5)).astype(bf16)
                else:
                    nk[hs, tl] = n
                    k = n * cols[GK, hs, :]
                    kT[h, :, tl] = k.astype(bf16)
                    kxT_n[h, tl, :] = jnp.concatenate([k, codes[:, tl]], 0).T.astype(bf16)
            return 0

        lax.fori_loop(0, NTL, head_loop, 0)

    QB = min(512, T)

    def attend(h, _):
        for r in range(T // QB):
            cs = slice(r * QB, (r + 1) * QB)
            e = jnp.exp(dot(kxT_n[h], qxT[h, :, cs])).astype(bf16)
            pT[h, :, cs] = e
            o = dot(vxT[h], e)
            inv = 1.0 / o[HEAD:HEAD + 1, :]
            o = o[:HEAD, :] * inv
            OT[h, :, cs] = o
            lT[h, 0:1, cs] = inv
        return 0

    lax.fori_loop(0, HEADS, attend, 0)
    for h in range(HEADS):
        mixT[h * HEAD:(h + 1) * HEAD, :] = OT[h].astype(bf16)

    copies[1].wait()
    wp[...] = wp_f[...].astype(bf16)
    midT[...] = dot(wp[...], mixT[:D, :], TN)

    def ln2_loop(t, _):
        tl = pl.ds(pl.multiple_of(t * LANES, LANES), LANES)
        m = midT[:, tl] + cols[BP] + xT[:, tl].astype(f32)
        midT[:, tl] = m
        mean = jnp.sum(m, 0, keepdims=True) * inv_d
        c = m - mean
        r = lax.rsqrt(jnp.sum(c * c, 0, keepdims=True) * inv_d + EPS)
        n2T[:D, tl] = (c * r * cols[N2G] + cols[N2B]).astype(bf16)
        stats[2:3, tl] = mean
        stats[3:4, tl] = r
        return 0

    lax.fori_loop(0, NTL, ln2_loop, 0)

    copies[2].wait()
    w1[...] = w1_f[...].astype(bf16)
    copies[3].wait()
    w2[...] = w2_f[...].astype(bf16)
    for f in range(NB):
        fs = slice(f * D, (f + 1) * D)
        preT[...] = dot(w1[:, fs], n2T[:D, :], TN)

        GB = 8

        def gelu_loop(i, _):
            rs = pl.ds(pl.multiple_of(i * 16, 16), 16)
            b = cols[B1 + f, rs, :]
            u = preT[rs, :] + jnp.concatenate([b] * NTL, 1)
            cdf, bell = normal_cdf(u)
            aT[rs, :] = (u * cdf).astype(bf16)
            gpT[rs, :] = (cdf + u * bell * 0.3989422804014327).astype(bf16)
            return 0

        lax.fori_loop(0, D // 16, gelu_loop, 0)
        preT[...] = dot(w2[fs, :], gmT[...])
        ghT[...] = (gpT[...].astype(f32) * preT[...]).astype(bf16)
        o = dot(w2[fs, :], aT[...], TN)
        d2 = dot(w1[:, fs], ghT[...])
        if f == 0:
            accT[...] = o
            dn2T[...] = d2
        else:
            accT[...] = accT[...] + o
            dn2T[...] = dn2T[...] + d2
        gw = dot(n2T[...], ghT[...], NT) * own
        g_fc1[:, fs] = gw[:D, :]
        g_vec[B1 + f:B1 + f + 1, :] = gw[D:D + 1, :]
        g_fc2[fs, :] = dot(aT[...], gmT[...], NT) * own
    g_vec[B2:B2 + 1, :] = dot(ones16, gmT[...], NT)[0:1, :] * own

    def lane_sums(j, value):
        part[j] = part[j] + value

    for j in range(6):
        part[j] = jnp.zeros((D, LANES), f32)

    for t in range(NTL):
        tl = slice(t * LANES, (t + 1) * LANES)
        m = midT[:, tl]
        out[tl, :] = (m + accT[:, tl] + cols[B2]).T.astype(bf16)
        r = stats[3:4, tl]
        n = (m - stats[2:3, tl]) * r
        dn = dn2T[:, tl]
        part[0] = part[0] + dn * n
        part[1] = part[1] + dn
        gn = dn * cols[N2G]
        m1 = jnp.sum(gn, 0, keepdims=True) * inv_d
        m2 = jnp.sum(gn * n, 0, keepdims=True) * inv_d
        gm = gmT[:, tl].astype(f32) + r * (gn - m1 - n * m2)
        gmidT[:, tl] = gm
        gbT[:, tl] = gm.astype(bf16)

    gw = dot(mixT[...], gbT[...], NT) * own
    g_proj[...] = gw[:D, :]
    g_vec[BP:BP + 1, :] = gw[D:D + 1, :]
    preT[...] = dot(wp[...], gbT[...])

    for h in range(HEADS):
        hs = slice(h * HEAD, (h + 1) * HEAD)
        inv = lT[h, 0:1, :]
        dol = (preT[hs, :].astype(bf16).astype(f32) * inv).astype(bf16)
        delta = -jnp.sum(dol.astype(f32) * OT[h], 0, keepdims=True)
        hi = delta.astype(bf16).astype(f32)
        lo = (delta - hi).astype(bf16).astype(f32)
        row = lax.broadcasted_iota(jnp.int32, (HEAD, T), 0)
        tail = jnp.where(row == 0, hi, jnp.where(row == 1, lo, jnp.where(row == 2, delta - hi - lo, 0.0)))
        doT[h, :HEAD, :] = dol
        doT[h, HEAD:, :] = tail.astype(bf16)

    def attend_back(h, _):
        for r in range(T // QB):
            cs = slice(r * QB, (r + 1) * QB)
            dsT[:, cs] = pT[h, :, cs] * dot(vx_n[h], doT[h, :, cs]).astype(bf16)
        preT[pl.ds(0, HEAD), :] = dot(kT[h], dsT[...])
        preT[pl.ds(HEAD, HEAD), :] = dot(qxT[h, :HEAD, :], dsT[...], NT)
        preT[pl.ds(2 * HEAD, HEAD), :] = dot(doT[h, :HEAD, :], pT[h], NT)
        hrow = pl.ds(pl.multiple_of(h * HEAD, HEAD), HEAD)

        for t in range(NTL):
            tl = slice(t * LANES, (t + 1) * LANES)
            for s in range(2):
                dy = preT[s * HEAD:(s + 1) * HEAD, tl]
                n = (nq if s == 0 else nk)[hrow, tl]
                if s == 0:
                    dy = dy * (HEAD ** -0.5)
                part[2 + s, hrow, :] = part[2 + s, hrow, :] + dy * n
                dy = dy * cols[GQ + s, hrow, :]
                r = rqk[s, h, 0:1, tl]
                m1 = jnp.sum(dy, 0, keepdims=True) * (1.0 / HEAD)
                m2 = jnp.sum(dy * n, 0, keepdims=True) * (1.0 / HEAD)
                gprT[s, hrow, tl] = (r * (dy - m1 - n * m2)).astype(bf16)
            gprT[2, hrow, tl] = preT[2 * HEAD:3 * HEAD, tl].astype(bf16)
        return 0

    lax.fori_loop(0, HEADS, attend_back, 0)

    for s in range(3):
        gw = dot(n1T[...], gprT[s], NT) * own
        g_qkv[:, s * D:(s + 1) * D] = gw[:D, :]
        g_vec[BQKV + s:BQKV + s + 1, :] = gw[D:D + 1, :]

    dn2T[...] = dot(wq[:, 0:D], gprT[0]) + dot(wq[:, D:2 * D], gprT[1]) + dot(wq[:, 2 * D:], gprT[2])
    for t in range(NTL):
        tl = slice(t * LANES, (t + 1) * LANES)
        r = stats[1:2, tl]
        n = (xT[:, tl].astype(f32) - stats[0:1, tl]) * r
        dn = dn2T[:, tl]
        part[4] = part[4] + dn * n
        part[5] = part[5] + dn
        gn = dn * cols[N1G]
        m1 = jnp.sum(gn, 0, keepdims=True) * inv_d
        m2 = jnp.sum(gn * n, 0, keepdims=True) * inv_d
        input_grad[tl, :] = (gmidT[:, tl] + r * (gn - m1 - n * m2)).T.astype(bf16)
    for j, where in ((0, N2G), (1, N2B), (2, GQ), (3, GK), (4, N1G), (5, N1B)):
        g_vec[where:where + 1, :] = jnp.sum(part[j].T, 0, keepdims=True) * own
    g_vec[B2 + 1:, :] = jnp.zeros((g_vec.shape[0] - B2 - 1, D), f32)


def layer(tokens, cotangent, seg, mask, bucket, loss_weights, n1g, n1b, wqkv, bqkv, gq, gk, wproj, bproj, n2g, n2b, wfc1, bfc1, wfc2, bfc2):
    T, D = tokens.shape
    FF = wfc1.shape[1]
    vm = pl.BlockSpec(memory_space=pltpu.VMEM)
    sm = pl.BlockSpec(memory_space=pltpu.SMEM)
    hb = pl.BlockSpec(memory_space=pl.ANY)
    S = jax.ShapeDtypeStruct
    V = pltpu.VMEM
    row = lambda v: v.reshape(1, -1)
    return pl.pallas_call(
        layer_kernel,
        out_shape=(S((T, D), bf16), S((T, D), bf16), S((D, 3 * D), f32), S((D, D), f32), S((D, FF), f32), S((FF, D), f32), S((16, D), f32)),
        in_specs=[vm, vm, vm, vm, sm, sm, vm, vm, hb, vm, vm, vm, hb, vm, vm, vm, hb, vm, hb, vm],
        out_specs=(vm,) * 7,
        scratch_shapes=[
            V((D, FF), bf16), V((FF, D), bf16), V((D, 3 * D), bf16), V((D, D), bf16),
            V((16, D, LANES), f32),
            V((HEAD, T), f32),
            V((D, T), bf16), V((D, T), bf16),
            V((D + 16, T), bf16), V((D + 16, T), bf16), V((D + 16, T), bf16),
            V((D, T), bf16),
            V((3, D, T), bf16),
            V((D, T), f32), V((D, T), f32), V((D, T), f32),
            V((HEADS, 2 * HEAD, T), bf16), V((HEADS, T, 2 * HEAD), bf16), V((HEADS, HEAD, T), bf16),
            V((HEADS, HEAD + 16, T), bf16), V((HEADS, T, 2 * HEAD), bf16),
            V((HEADS, T, T), bf16),
            V((HEADS, HEAD, T), f32), V((HEADS, 8, T), f32), V((HEADS, 2 * HEAD, T), bf16),
            V((D, T), f32), V((D, T), f32), V((D, T), f32), V((D, T), f32),
            V((T, T), bf16),
            V((8, T), f32), V((2, HEADS, 8, T), f32), V((6, D, LANES), f32),
            pltpu.SemaphoreType.DMA((8,)),
        ],
        compiler_params=pltpu.CompilerParams(vmem_limit_bytes=63 * 2 ** 20),
        name="layer",
    )(tokens, cotangent, row(seg), row(mask), bucket, loss_weights, n1g, n1b, wqkv, bqkv, gq, gk, wproj, bproj, n2g, n2b, wfc1, bfc1, wfc2, bfc2)


def shards(*args):
    out, input_grad, g_qkv, g_proj, g_fc1, g_fc2, g_vec = layer(*args)
    g_qkv, g_proj, g_fc1, g_fc2, g_vec = lax.psum((g_qkv, g_proj, g_fc1, g_fc2, g_vec), ("wide", "narrow"))
    NB = g_fc1.shape[1] // g_fc1.shape[0]
    v = [g_vec[j] for j in range(11 + NB)]
    return (
        out, input_grad, v[0], v[1], g_qkv, jnp.concatenate(v[2:5]), v[5], v[6], g_proj, v[7], v[8], v[9],
        g_fc1, jnp.concatenate(v[10:10 + NB]), g_fc2, v[10 + NB],
    )


def solution(mesh):
    split = P(("wide", "narrow"))
    return jax.shard_map(
        shards,
        mesh=mesh,
        in_specs=(split, split, split, split, P("wide")) + (P(),) * 15,
        out_specs=(split, split) + (P(),) * 14,
        check_vma=False,
    )
```

```python
import functools

import jax
import jax.numpy as jnp
from jax import lax
from jax.experimental import pallas as pl
from jax.experimental.pallas import tpu as pltpu
from jax.sharding import PartitionSpec as P

HEADS = 6
HEAD = 64
EPS = 1e-06
CODE = 128.0
LANES = 128
bf16 = jnp.bfloat16
f32 = jnp.float32

NN = ((1,), (0,))
NT = ((1,), (1,))
TN = ((0,), (0,))


def dot(left, right, dims=NN):
    return lax.dot_general(left, right, (dims, ((), ())), preferred_element_type=f32)


def normal_cdf(u):
    z = jnp.abs(u) * 0.7071067811865476
    t = 1.0 / (1.0 + 0.3275911 * z)
    bell = jnp.exp(-(z * z))
    poly = t * (0.254829592 + t * (-0.284496736 + t * (1.421413741 + t * (-1.453152027 + t * 1.061405429))))
    half = 0.5 * poly * bell
    return jnp.where(u < 0, half, 1.0 - half), bell


MESH = pl.DeviceIdType.MESH
ORDER = (("x", "y", 1, 2, 3), ("y", 1, 2, 3, "xe"), (1, 2, 3, "xe", "ye"))
FIRST = (0, 192, 408)
ARRIVE = 672
STAGES = 12


class Links:
    def __init__(self, G, F, R, Q, send, recv, local):
        self.G, self.F, self.R, self.Q = G, F, R, Q
        self.send_sem, self.recv_sem, self.local = send, recv, local
        w = lax.axis_index("wide")
        self.w, self.z = w, lax.axis_index("narrow")
        self.core, self.bit = lax.rem(w, 2), {"x": lax.rem(w // 2, 2), "y": w // 4}
        self.flip = {"core": 1 - 2 * self.core, "x": 2 - 4 * self.bit["x"], "y": 4 - 8 * self.bit["y"]}
        self.ends = (self.z == 0) | (self.z == 3)
        self.end = self.z // 3

    def partner(self, axis):
        return (self.w + self.flip[axis], self.z)

    def barrier(self):
        sem = pltpu.get_barrier_semaphore()
        peers = [self.partner("core"), self.partner("x"), self.partner("y")]
        peers += [(self.w, lax.rem(self.z + d, 4)) for d in (1, 2, 3)]
        for p in peers:
            pl.semaphore_signal(sem, inc=1, device_id=p, device_id_type=MESH)
        pl.semaphore_wait(sem, len(peers))

    def regions(self, g):
        start, n = self.core * 192, 192
        out = []
        for step in ORDER[g]:
            out.append((start, n))
            if step in (1, 2):
                continue
            n //= 2
            start = start + (self.end if step == 3 else self.bit[step[0]]) * n
        out.append((start, n))
        return out

    def rows(self, start, n):
        return pl.ds(pl.multiple_of(start, 8), n)

    def copy(self, src, dst, unit, k, to):
        u = unit[0]
        return pltpu.make_async_remote_copy(
            src_ref=src, dst_ref=dst, send_sem=self.send_sem.at[u, k], recv_sem=self.recv_sem.at[u, k],
            device_id=to, device_id_type=MESH)

    def chunks(self, unit):
        return pl.ds(unit[1], unit[2])

    def arrival(self, unit, g, step, up=True):
        want = step[0] if isinstance(step, str) else ("u" if up else "d")
        at, n = FIRST[g], 192
        for st in ORDER[g]:
            if st in (1, 2):
                continue
            n //= 2
            for name in (("u", "d") if st == 3 else (st[0],)):
                if name == want:
                    return at, n
                at += n

    def arrived(self, unit, at, n):
        return self.Q.at[unit[0] % self.Q.shape[0], pl.ds(0, unit[2]), pl.ds(at, n), :]

    def core_copy(self, unit, gather):
        c = self.chunks(unit)
        to = self.partner("core")
        if gather:
            mine = self.rows(self.core * 192, 192)
            return self.copy(self.F.at[c, :, mine, :], self.F.at[c, :, mine, :], unit, 25, to)
        other = self.rows((1 - self.core) * 192, 192)
        return self.copy(self.G.at[c, :, other, :], self.R.at[unit[0] % self.R.shape[0], pl.ds(0, unit[2])], unit, 0, to)

    def half_copy(self, unit, g, j, gather):
        step = ORDER[g][j]
        start, n = self.regions(g)[j]
        b, half, c = self.bit[step[0]], n // 2, self.chunks(unit)
        k = 1 + 8 * g + (4 if gather else 0) + (0 if step[0] == "x" else 1)
        to = self.partner(step[0])
        if gather:
            mine = self.rows(start + b * half, half)
            return self.copy(self.F.at[c, g, mine, :], self.F.at[c, g, mine, :], unit, k, to)
        other = self.rows(start + (1 - b) * half, half)
        return self.copy(self.G.at[c, g, other, :], self.arrived(unit, *self.arrival(unit, g, step)), unit, k, to)

    def line_copy(self, unit, g, h, gather, up):
        start, n = self.regions(g)[ORDER[g].index(h)]
        half, c = n // 2, self.chunks(unit)
        part = self.rows(start + (half if up != gather else 0), half)
        k = 1 + 8 * g + (4 if gather else 0) + (2 if up else 3)
        to = (self.w, lax.rem(self.z + (1 if up else 3), 4))
        if gather:
            return self.copy(self.F.at[c, g, part, :], self.F.at[c, g, part, :], unit, k, to)
        return self.copy(self.G.at[c, g, part, :], self.arrived(unit, *self.arrival(unit, g, h, up)), unit, k, to)

    def add(self, unit, g, start, at, n):
        r = self.rows(start, n)
        q = unit[0] % self.Q.shape[0]
        for i in range(unit[2]):
            c = unit[1] + i
            self.G[c, g, r, :] = self.G[c, g, r, :] + self.Q[q, i, pl.ds(at, n), :]

    def send(self, unit, g, j, gather):
        step = ORDER[g][j]
        if isinstance(step, str):
            c = self.half_copy(unit, g, j, gather)
            if len(step) == 2:
                pl.when(self.ends)(c.start)
            else:
                c.start()
            return
        pl.when(self.z == step - 1)(self.line_copy(unit, g, step, gather, True).start)
        pl.when(self.z == 4 - step)(self.line_copy(unit, g, step, gather, False).start)

    def wait(self, unit, g, j, gather):
        step = ORDER[g][j]
        start, n = self.regions(g)[j]
        if isinstance(step, str):
            c = self.half_copy(unit, g, j, gather)

            def finish():
                c.wait_recv()
                if not gather:
                    at, size = self.arrival(unit, g, step)
                    self.add(unit, g, start + self.bit[step[0]] * size, at, size)
                c.wait_send()

            if len(step) == 2:
                pl.when(self.ends)(finish)
            else:
                finish()
            return
        for up in (True, False):
            c = self.line_copy(unit, g, step, gather, up)

            def finish(c=c, up=up):
                c.wait_recv()
                if not gather:
                    at, size = self.arrival(unit, g, step, up)
                    self.add(unit, g, start + (n // 2 if up else 0), at, size)

            pl.when(self.z == (step if up else 3 - step))(finish)
            pl.when(self.z == (step - 1 if up else 4 - step))(c.wait_send)

    def keep(self, unit, g):
        r = self.rows(*self.regions(g)[5])
        c = self.chunks(unit)
        return pltpu.make_async_copy(self.G.at[c, g, r, :], self.F.at[c, g, r, :], self.local.at[unit[1], g])

    def gather_step(self, g, stage):
        line = [j for j in range(5) if not isinstance(ORDER[g][j], str)]
        order = list(range(4, line[-1], -1)) + line + list(range(line[0] - 1, -1, -1))
        return order[stage - 6]

    def begin(self, unit):
        self.core_copy(unit, False).start()

    def stage(self, unit, k):
        if k == 0:
            c = self.core_copy(unit, False)
            c.wait_recv()
            mine = self.rows(self.core * 192, 192)
            for g in range(3):
                for i in range(unit[2]):
                    self.G[unit[1] + i, g, mine, :] = self.G[unit[1] + i, g, mine, :] + self.R[unit[0] % self.R.shape[0], i, g]
                self.send(unit, g, 0, False)
            c.wait_send()
        elif k < 5:
            for g in range(3):
                self.wait(unit, g, k - 1, False)
                self.send(unit, g, k, False)
        elif k == 5:
            for g in range(3):
                self.wait(unit, g, 4, False)

            @pl.when(self.ends)
            def _():
                for g in range(3):
                    self.keep(unit, g).start()
                for g in range(3):
                    self.keep(unit, g).wait()

            for g in range(3):
                self.send(unit, g, self.gather_step(g, 6), True)
        elif k < 10:
            for g in range(3):
                self.wait(unit, g, self.gather_step(g, k), True)
                self.send(unit, g, self.gather_step(g, k + 1), True)
        elif k == 10:
            for g in range(3):
                self.wait(unit, g, self.gather_step(g, 10), True)
            self.core_copy(unit, True).start()
        else:
            self.core_copy(unit, True).wait()


class Flow:
    def __init__(self, links):
        self.links, self.active, self.count = links, [], 0

    def ready(self, first, number):
        if self.links is None:
            return
        unit = (self.count, first, number)
        self.count += 1
        self.links.begin(unit)
        self.active.append([unit, 0])

    def tick(self):
        for entry in list(self.active):
            self.links.stage(*entry)
            entry[1] += 1
            if entry[1] == STAGES:
                self.active.remove(entry)

    def finish(self):
        while self.active:
            self.tick()


class VectorSum:
    def __init__(self, links, V, VR, send, recv):
        self.links, self.V, self.VR, self.sems, self.at = links, V, VR, (send, recv), 0

    def copies(self, j):
        L = self.links
        send, recv = self.sems
        if j < 3:
            to = [(j, L.partner(("core", "x", "y")[j]))]
        else:
            to = [(2 + d, (L.w, lax.rem(L.z + d, 4))) for d in (1, 2, 3)]
        return [pltpu.make_async_remote_copy(
            src_ref=self.V.at[j], dst_ref=self.VR.at[r], send_sem=send.at[r], recv_sem=recv.at[r],
            device_id=p, device_id_type=MESH) for r, p in to]

    def begin(self):
        self.copies(0)[0].start()

    def tick(self):
        j = self.at
        if j > 3:
            return
        self.at += 1
        V, VR = self.V, self.VR
        cs = self.copies(j)
        for c in cs:
            c.wait_recv()
        if j < 3:
            V[j + 1] = V[j] + VR[j]
        else:
            total = None
            for zz in range(4):
                d = lax.rem(self.links.z - zz + 4, 4)
                v = jnp.where(d == 0, V[3], jnp.where(d == 1, VR[3], jnp.where(d == 2, VR[4], VR[5])))
                total = v if total is None else total + v
            V[4] = total
        for c in cs:
            c.wait_send()
        if j < 3:
            for c in self.copies(j + 1):
                c.start()


def layer_kernel(
    linked, tokens, cotangent, seg, mask, bucket, loss_weights,
    n1g, n1b, wqkv, bqkv, gq, gk, wproj, bproj, n2g, n2b, wfc1, bfc1, wfc2, bfc2,
    out, input_grad, F, vec_out,
    w1, w2, wq, wp,
    cols, codes, xT, gmT, n1T, mixT, n2T, gbT, gprT,
    preT, nq, nk, qxT, kxT_n, kT, vxT, vx_n, pT, OT, lT, doT, midT, accT, dn2T, dsT,
    stats, rqk, part, G, V, VR, R, Q, local, sems, send, recv, vsend, vrecv,
):
    T = tokens.shape[0]
    D = tokens.shape[1]
    FF = wfc1.shape[1]
    NB = FF // D
    NTL = T // LANES
    aT, ghT, gpT = dsT.at[:D], dsT.at[D:2 * D], gbT

    gmidT = accT
    QKV, PROJ = 2 * NB + 1, 2 * NB
    where = {}
    for s in range(3):
        for p in range(3):
            where[QKV + p, s] = wqkv.at[:, pl.ds(s * D + p * LANES, LANES)]
        where[PROJ, s] = wproj.at[:, pl.ds(s * LANES, LANES)]
        for f in range(NB):
            where[2 * f, s] = wfc2.at[pl.ds(f * D, D), pl.ds(s * LANES, LANES)]
            where[2 * f + 1, s] = wfc1.at[:, pl.ds(f * D + s * LANES, LANES)]

    def fetch(c, s):
        return pltpu.make_async_copy(where[c, s], G.at[c, s], local.at[c, s])

    tok_copy = pltpu.make_async_copy(tokens, dsT.at[:, :D], sems.at[0])
    cot_copy = pltpu.make_async_copy(cotangent, dsT.at[:, D:2 * D], sems.at[1])
    tok_copy.start()
    cot_copy.start()
    for c in [QKV, QKV + 1, QKV + 2, PROJ] + list(range(2 * NB)):
        for s in range(3):
            fetch(c, s).start()

    links = Links(G, F, R, Q, send, recv, local) if linked else None
    flow = Flow(links)

    def put(c, s, gw):
        G[c, s] = gw

    def put_vec(j, row):
        for s in range(3):
            V[0, 3 * j + s:3 * j + s + 1, :] = row[:, s * LANES:(s + 1) * LANES]

    own = jnp.where(bucket[0] == 0, loss_weights[0], loss_weights[1]).astype(f32)
    devices = lax.axis_size("wide") * lax.axis_size("narrow")
    own = own / devices

    rows = [n1g[...], n1b[...]] + [bqkv[i * D:(i + 1) * D] for i in range(3)] + [gq[...], gk[...], bproj[...], n2g[...], n2b[...]]
    rows += [bfc1[i * D:(i + 1) * D] for i in range(NB)] + [bfc2[...]]
    rows = [v.reshape(1, D) for v in rows]
    N1G, N1B, BQKV, GQ, GK, BP, N2G, N2B, B1 = 0, 1, 2, 5, 6, 7, 8, 9, 10
    B2 = 10 + NB
    stacked = jnp.concatenate(rows + [jnp.zeros((LANES - len(rows), D), f32)], 0)
    colmat = stacked.T
    for j in range(len(rows)):
        cols[j] = jnp.broadcast_to(colmat[:, j:j + 1], (D, LANES))

    segrow = seg[...]
    sub = lax.broadcasted_iota(jnp.int32, (HEAD, T), 0)
    bits = jnp.where((jnp.broadcast_to(segrow, (HEAD, T)) & (1 << jnp.minimum(sub, 12))) != 0, 1.0, -1.0)
    codes[...] = jnp.where(sub < 10, bits, jnp.where(sub == 10, 1.0, 0.0))
    coderow = jnp.where(sub < 10, CODE * bits, jnp.where(sub == 10, -10.0 * CODE, 0.0)).astype(bf16)
    for h in range(HEADS):
        qxT[h, HEAD:, :] = coderow
        vxT[h, HEAD:, :] = jnp.where(lax.broadcasted_iota(jnp.int32, (16, T), 0) == 0, 1.0, 0.0).astype(bf16)

    maskrow = mask[...].astype(f32)
    ones16 = jnp.where(lax.broadcasted_iota(jnp.int32, (16, T), 0) == 0, 1.0, 0.0).astype(bf16)
    n1T[D:, :] = ones16
    n2T[D:, :] = ones16
    mixT[D:, :] = ones16

    inv_d = 1.0 / D

    tok_copy.wait()
    cot_copy.wait()
    for t in range(NTL):
        tl = slice(t * LANES, (t + 1) * LANES)
        x = dsT[tl, :D].astype(f32).T
        xT[:, tl] = x.astype(bf16)
        mean = jnp.sum(x, 0, keepdims=True) * inv_d
        c = x - mean
        r = lax.rsqrt(jnp.sum(c * c, 0, keepdims=True) * inv_d + EPS)
        n1T[:D, tl] = (c * r * cols[N1G] + cols[N1B]).astype(bf16)
        stats[0:1, tl] = mean
        stats[1:2, tl] = r
        gmT[:, tl] = (dsT[tl, D:2 * D].astype(f32).T * maskrow[:, tl]).astype(bf16)

    for p in range(3):
        for s in range(3):
            fetch(QKV + p, s).wait()
            wq[:, s * D + p * LANES:s * D + (p + 1) * LANES] = G[QKV + p, s].astype(bf16)
    for s in range(3):
        preT[...] = dot(wq[:, s * D:(s + 1) * D], n1T[:D, :], TN)
        ext = jnp.where(lax.broadcasted_iota(jnp.int32, (HEAD, LANES), 0) < 3, 1.0, 0.0)

        def head_loop(t, _):
            tl = pl.ds(pl.multiple_of(t * LANES, LANES), LANES)
            for h in range(HEADS):
                hs = slice(h * HEAD, (h + 1) * HEAD)
                v = preT[hs, tl] + cols[BQKV + s, hs, :]
                if s == 2:
                    vxT[h, :HEAD, tl] = v.astype(bf16)
                    vx_n[h, tl, :] = jnp.concatenate([v, ext], 0).T.astype(bf16)
                    continue
                mean = jnp.sum(v, 0, keepdims=True) * (1.0 / HEAD)
                c = v - mean
                r = lax.rsqrt(jnp.sum(c * c, 0, keepdims=True) * (1.0 / HEAD) + EPS)
                n = c * r
                rqk[s, h, 0:1, tl] = r
                if s == 0:
                    nq[hs, tl] = n
                    qxT[h, :HEAD, tl] = (n * cols[GQ, hs, :] * (HEAD ** -0.5)).astype(bf16)
                else:
                    nk[hs, tl] = n
                    k = n * cols[GK, hs, :]
                    kT[h, :, tl] = k.astype(bf16)
                    kxT_n[h, tl, :] = jnp.concatenate([k, codes[:, tl]], 0).T.astype(bf16)
            return 0

        lax.fori_loop(0, NTL, head_loop, 0)

    QB = min(512, T)

    def attend(h, _):
        for r in range(T // QB):
            cs = slice(r * QB, (r + 1) * QB)
            e = jnp.exp(dot(kxT_n[h], qxT[h, :, cs])).astype(bf16)
            pT[h, :, cs] = e
            o = dot(vxT[h], e)
            inv = 1.0 / o[HEAD:HEAD + 1, :]
            o = o[:HEAD, :] * inv
            OT[h, :, cs] = o
            lT[h, 0:1, cs] = inv
        return 0

    lax.fori_loop(0, HEADS, attend, 0)
    for h in range(HEADS):
        mixT[h * HEAD:(h + 1) * HEAD, :] = OT[h].astype(bf16)

    for s in range(3):
        fetch(PROJ, s).wait()
        wp[:, s * LANES:(s + 1) * LANES] = G[PROJ, s].astype(bf16)
    midT[...] = dot(wp[...], mixT[:D, :], TN)

    def ln2_loop(t, _):
        tl = pl.ds(pl.multiple_of(t * LANES, LANES), LANES)
        m = midT[:, tl] + cols[BP] + xT[:, tl].astype(f32)
        midT[:, tl] = m
        mean = jnp.sum(m, 0, keepdims=True) * inv_d
        c = m - mean
        r = lax.rsqrt(jnp.sum(c * c, 0, keepdims=True) * inv_d + EPS)
        n2T[:D, tl] = (c * r * cols[N2G] + cols[N2B]).astype(bf16)
        stats[2:3, tl] = mean
        stats[3:4, tl] = r
        return 0

    lax.fori_loop(0, NTL, ln2_loop, 0)

    if linked:
        links.barrier()
    for f in range(NB):
        for s in range(3):
            fetch(2 * f, s).wait()
            fetch(2 * f + 1, s).wait()
            w2[f * D:(f + 1) * D, s * LANES:(s + 1) * LANES] = G[2 * f, s].astype(bf16)
            w1[:, f * D + s * LANES:f * D + (s + 1) * LANES] = G[2 * f + 1, s].astype(bf16)
    for f in range(NB):
        fs = slice(f * D, (f + 1) * D)
        preT[...] = dot(w1[:, fs], n2T[:D, :], TN)

        GB = 8

        def gelu_loop(i, _):
            rs = pl.ds(pl.multiple_of(i * 16, 16), 16)
            b = cols[B1 + f, rs, :]
            u = preT[rs, :] + jnp.concatenate([b] * NTL, 1)
            cdf, bell = normal_cdf(u)
            aT[rs, :] = (u * cdf).astype(bf16)
            gpT[rs, :] = (cdf + u * bell * 0.3989422804014327).astype(bf16)
            return 0

        lax.fori_loop(0, D // 16, gelu_loop, 0)
        flow.tick()
        preT[...] = dot(w2[fs, :], gmT[...])
        ghT[...] = (gpT[...].astype(f32) * preT[...]).astype(bf16)
        o = dot(w2[fs, :], aT[...], TN)
        d2 = dot(w1[:, fs], ghT[...])
        if f == 0:
            accT[...] = o
            dn2T[...] = d2
        else:
            accT[...] = accT[...] + o
            dn2T[...] = dn2T[...] + d2
        flow.tick()
        gw = dot(n2T[...], ghT[...], NT) * own
        for s in range(3):
            G[2 * f + 1, s] = gw[:D, s * LANES:(s + 1) * LANES]
        put_vec(B1 + f, gw[D:D + 1, :])
        gw = dot(aT[...], gmT[...], NT) * own
        for s in range(3):
            G[2 * f, s] = gw[:, s * LANES:(s + 1) * LANES]
        flow.ready(2 * f, 2)
    put_vec(B2, dot(ones16, gmT[...], NT)[0:1, :] * own)

    def lane_sums(j, value):
        part[j] = part[j] + value

    for j in range(6):
        part[j] = jnp.zeros((D, LANES), f32)

    for t in range(NTL):
        tl = slice(t * LANES, (t + 1) * LANES)
        m = midT[:, tl]
        dsT[tl, :D] = (m + accT[:, tl] + cols[B2]).T.astype(bf16)
        r = stats[3:4, tl]
        n = (m - stats[2:3, tl]) * r
        dn = dn2T[:, tl]
        part[0] = part[0] + dn * n
        part[1] = part[1] + dn
        gn = dn * cols[N2G]
        m1 = jnp.sum(gn, 0, keepdims=True) * inv_d
        m2 = jnp.sum(gn * n, 0, keepdims=True) * inv_d
        gm = gmT[:, tl].astype(f32) + r * (gn - m1 - n * m2)
        gmidT[:, tl] = gm
        gbT[:, tl] = gm.astype(bf16)

    out_copy = pltpu.make_async_copy(dsT.at[:, :D], out, sems.at[0])
    out_copy.start()
    flow.tick()
    gw = dot(mixT[...], gbT[...], NT) * own
    for s in range(3):
        G[PROJ, s] = gw[:D, s * LANES:(s + 1) * LANES]
    flow.ready(PROJ, 1)
    put_vec(BP, gw[D:D + 1, :])
    preT[...] = dot(wp[...], gbT[...])

    for h in range(HEADS):
        hs = slice(h * HEAD, (h + 1) * HEAD)
        inv = lT[h, 0:1, :]
        dol = (preT[hs, :].astype(bf16).astype(f32) * inv).astype(bf16)
        delta = -jnp.sum(dol.astype(f32) * OT[h], 0, keepdims=True)
        hi = delta.astype(bf16).astype(f32)
        lo = (delta - hi).astype(bf16).astype(f32)
        row = lax.broadcasted_iota(jnp.int32, (HEAD, T), 0)
        tail = jnp.where(row == 0, hi, jnp.where(row == 1, lo, jnp.where(row == 2, delta - hi - lo, 0.0)))
        doT[h, :HEAD, :] = dol
        doT[h, HEAD:, :] = tail.astype(bf16)

    out_copy.wait()
    flow.tick()

    def attend_back(h, _):
        for r in range(T // QB):
            cs = slice(r * QB, (r + 1) * QB)
            dsT[:, cs] = pT[h, :, cs] * dot(vx_n[h], doT[h, :, cs]).astype(bf16)
        preT[pl.ds(0, HEAD), :] = dot(kT[h], dsT[...])
        preT[pl.ds(HEAD, HEAD), :] = dot(qxT[h, :HEAD, :], dsT[...], NT)
        preT[pl.ds(2 * HEAD, HEAD), :] = dot(doT[h, :HEAD, :], pT[h], NT)
        hrow = slice(h * HEAD, (h + 1) * HEAD)

        for t in range(NTL):
            tl = slice(t * LANES, (t + 1) * LANES)
            for s in range(2):
                dy = preT[s * HEAD:(s + 1) * HEAD, tl]
                n = (nq if s == 0 else nk)[hrow, tl]
                if s == 0:
                    dy = dy * (HEAD ** -0.5)
                part[2 + s, hrow, :] = part[2 + s, hrow, :] + dy * n
                dy = dy * cols[GQ + s, hrow, :]
                r = rqk[s, h, 0:1, tl]
                m1 = jnp.sum(dy, 0, keepdims=True) * (1.0 / HEAD)
                m2 = jnp.sum(dy * n, 0, keepdims=True) * (1.0 / HEAD)
                gprT[s, hrow, tl] = (r * (dy - m1 - n * m2)).astype(bf16)
            gprT[2, hrow, tl] = preT[2 * HEAD:3 * HEAD, tl].astype(bf16)
        return 0

    for p in range(HEADS // 2):
        for h in (2 * p, 2 * p + 1):
            attend_back(h, 0)
            flow.tick()
        ps = slice(p * LANES, (p + 1) * LANES)
        for s in range(3):
            gw = dot(n1T[...], gprT[s, ps, :], NT) * own
            G[QKV + p, s] = gw[:D, :]
            V[0, 3 * (BQKV + s) + p:3 * (BQKV + s) + p + 1, :] = gw[D:D + 1, :]
        flow.ready(QKV + p, 1)

    dn2T[...] = dot(wq[:, 0:D], gprT[0]) + dot(wq[:, D:2 * D], gprT[1]) + dot(wq[:, 2 * D:], gprT[2])
    flow.tick()
    for t in range(NTL):
        tl = slice(t * LANES, (t + 1) * LANES)
        r = stats[1:2, tl]
        n = (xT[:, tl].astype(f32) - stats[0:1, tl]) * r
        dn = dn2T[:, tl]
        part[4] = part[4] + dn * n
        part[5] = part[5] + dn
        gn = dn * cols[N1G]
        m1 = jnp.sum(gn, 0, keepdims=True) * inv_d
        m2 = jnp.sum(gn * n, 0, keepdims=True) * inv_d
        dsT[tl, D:2 * D] = (gmidT[:, tl] + r * (gn - m1 - n * m2)).T.astype(bf16)
    grad_copy = pltpu.make_async_copy(dsT.at[:, D:2 * D], input_grad, sems.at[1])
    grad_copy.start()
    for j, at in ((0, N2G), (1, N2B), (2, GQ), (3, GK), (4, N1G), (5, N1B)):
        put_vec(at, jnp.sum(part[j].T, 0, keepdims=True) * own)
    used = 3 * (B2 + 1)
    V[0, used:, :] = jnp.zeros((V.shape[1] - used, LANES), f32)
    if linked:
        vectors = VectorSum(links, V, VR, vsend, vrecv)
        vectors.begin()
        while flow.active:
            flow.tick()
            vectors.tick()
        vec_out[...] = V[4]
    else:
        whole = pltpu.make_async_copy(G, F, local.at[0, 0])
        whole.start()
        vec_out[...] = V[0]
        whole.wait()
    grad_copy.wait()


def layer(linked, tokens, cotangent, seg, mask, bucket, loss_weights, n1g, n1b, wqkv, bqkv, gq, gk, wproj, bproj, n2g, n2b, wfc1, bfc1, wfc2, bfc2):
    T, D = tokens.shape
    FF = wfc1.shape[1]
    vm = pl.BlockSpec(memory_space=pltpu.VMEM)
    sm = pl.BlockSpec(memory_space=pltpu.SMEM)
    hb = pl.BlockSpec(memory_space=pl.ANY)
    S = jax.ShapeDtypeStruct
    V = pltpu.VMEM
    row = lambda v: v.reshape(1, -1)
    NB = FF // D
    NC = 2 * NB + 4
    R_SLOTS, Q_SLOTS, UNITS, PART = (2, 4, 8, 2) if linked else (1, 1, 1, 1)
    return pl.pallas_call(
        functools.partial(layer_kernel, linked),
        out_shape=(S((T, D), bf16), S((T, D), bf16), S((NC, 3, D, LANES), f32), S((48, LANES), f32)),
        in_specs=[hb, hb, vm, vm, sm, sm, vm, vm, hb, vm, vm, vm, hb, vm, vm, vm, hb, vm, hb, vm],
        out_specs=(hb, hb, hb, vm),
        scratch_shapes=[
            V((D, FF), bf16), V((FF, D), bf16), V((D, 3 * D), bf16), V((D, D), bf16),
            V((11 + NB, D, LANES), f32),
            V((HEAD, T), f32),
            V((D, T), bf16), V((D, T), bf16),
            V((D + 16, T), bf16), V((D + 16, T), bf16), V((D + 16, T), bf16),
            V((D, T), bf16),
            V((3, D, T), bf16),
            V((D, T), f32), V((D, T), f32), V((D, T), f32),
            V((HEADS, 2 * HEAD, T), bf16), V((HEADS, T, 2 * HEAD), bf16), V((HEADS, HEAD, T), bf16),
            V((HEADS, HEAD + 16, T), bf16), V((HEADS, T, 2 * HEAD), bf16),
            V((HEADS, T, T), bf16),
            V((HEADS, HEAD, T), f32), V((HEADS, 8, T), f32), V((HEADS, 2 * HEAD, T), bf16),
            V((D, T), f32), V((D, T), f32), V((D, T), f32),
            V((T, T), bf16),
            V((8, T), f32), V((2, HEADS, 8, T), f32), V((6, D, LANES), f32),
            V((NC, 3, D, LANES), f32), V((5, 48, LANES), f32), V((6, 48, LANES), f32),
            V((R_SLOTS, PART, 3, 192, LANES), f32), V((Q_SLOTS, PART, ARRIVE, LANES), f32),
            pltpu.SemaphoreType.DMA((NC, 3)), pltpu.SemaphoreType.DMA((2,)),
            pltpu.SemaphoreType.DMA((UNITS, 26)), pltpu.SemaphoreType.DMA((UNITS, 26)),
            pltpu.SemaphoreType.DMA((6,)), pltpu.SemaphoreType.DMA((6,)),
        ],
        compiler_params=pltpu.CompilerParams(
            vmem_limit_bytes=int(63.9 * 2 ** 20), has_side_effects=linked, **({"collective_id": 0} if linked else {})),
        name="layer",
    )(tokens, cotangent, row(seg), row(mask), bucket, loss_weights, n1g, n1b, wqkv, bqkv, gq, gk, wproj, bproj, n2g, n2b, wfc1, bfc1, wfc2, bfc2)


def arrange_kernel(NB, F, vec, *refs):
    (n1g, n1b, qkv, bqkv, gq, gk, proj, bproj, n2g, n2b, fc1, bfc1, fc2, bfc2), held, come, gone = refs[:14], *refs[14:]
    D = F.shape[2]
    copies = []
    for s in range(3):
        lanes = slice(s * LANES, (s + 1) * LANES)
        for f in range(NB):
            copies.append((2 * f, s, fc2.at[pl.ds(f * D, D), lanes]))
            copies.append((2 * f + 1, s, fc1.at[:, pl.ds(f * D + s * LANES, LANES)]))
        copies.append((2 * NB, s, proj.at[:, lanes]))
        for p in range(3):
            copies.append((2 * NB + 1 + p, s, qkv.at[:, pl.ds(s * D + p * LANES, LANES)]))
    copies.sort(key=lambda c: c[:2])
    reads = [pltpu.make_async_copy(F.at[c], held.at[c], come.at[c]) for c in range(F.shape[0])]
    for c in reads:
        c.start()
    writes = []
    for c, s, ref in copies:
        if s == 0:
            reads[c].wait()
        writes.append(pltpu.make_async_copy(held.at[c, s], ref, gone.at[c, s]))
        writes[-1].start()
    at = 0
    for ref in (n1g, n1b, bqkv, gq, gk, bproj, n2g, n2b, bfc1, bfc2):
        for i in range(ref.shape[0] // LANES):
            ref[i * LANES:(i + 1) * LANES] = vec[at]
            at += 1
    for c in writes:
        c.wait()


def arrange(F, vec, D, FF):
    vm = pl.BlockSpec(memory_space=pltpu.VMEM)
    hb = pl.BlockSpec(memory_space=pl.ANY)
    v = lambda n: jax.ShapeDtypeStruct((n,), f32)
    m = lambda a, b: jax.ShapeDtypeStruct((a, b), f32)
    shapes = (v(D), v(D), m(D, 3 * D), v(3 * D), v(D), v(D), m(D, D), v(D), v(D), v(D), m(D, FF), v(FF), m(FF, D), v(D))
    return pl.pallas_call(
        functools.partial(arrange_kernel, FF // D),
        out_shape=shapes,
        in_specs=[hb, vm],
        out_specs=tuple(vm if len(x.shape) == 1 else hb for x in shapes),
        scratch_shapes=[pltpu.VMEM(F.shape, f32), pltpu.SemaphoreType.DMA((F.shape[0],)), pltpu.SemaphoreType.DMA((F.shape[0], 3))],
        compiler_params=pltpu.CompilerParams(vmem_limit_bytes=16 * 2 ** 20),
        name="arrange",
    )(F, vec)


def shards(linked, *args):
    out, input_grad, F, vec = layer(linked, *args)
    if not linked:
        F, vec = lax.psum((F, vec), ("wide", "narrow"))
    return (out, input_grad) + tuple(arrange(F, vec, args[0].shape[1], args[16].shape[1]))


def solution(mesh):
    split = P(("wide", "narrow"))
    linked = (mesh.shape["wide"], mesh.shape["narrow"]) == (8, 4)
    return jax.shard_map(
        functools.partial(shards, linked),
        mesh=mesh,
        in_specs=(split, split, split, split, P("wide")) + (P(),) * 15,
        out_specs=(split, split) + (P(),) * 14,
        check_vma=False,
    )
```
